32 devices in a mesh: groups: 2 (over x), tensor: 16 (over z, y, core).
Axes of the slice: x: 2, y: 2, z: 4, core: 2. Of those that a mesh axis runs over, the one named last changes fastest.
Arguments:
- tokens: bfloat16 [1024, 2560], P(('groups', 'tensor')), parts along dimension 0, may hold values from -6 to 6
- grad_out: bfloat16 [1024, 2560], P(('groups', 'tensor')), parts along dimension 0, may hold values from -6 to 6
- gate_base: bfloat16 [2560, 13824], P(None, 'tensor'), may hold values from -0.125 to 0.125
- up_base: bfloat16 [2560, 13824], P(None, 'tensor'), may hold values from -0.125 to 0.125
- down_base: bfloat16 [13824, 2560], P('tensor'), may hold values from -0.0546875 to 0.0546875
- gate_delta: bfloat16 [2, 2560, 13824], P(None, None, 'tensor'), may hold values from -0.03125 to 0.03125
- up_delta: bfloat16 [2, 2560, 13824], P(None, None, 'tensor'), may hold values from -0.03125 to 0.03125
- down_delta: bfloat16 [2, 13824, 2560], P(None, 'tensor'), may hold values from -0.015625 to 0.015625
- offsets: int32 [3, 16], P(None, 'tensor'), may hold values from 0 to 1073741823
- seeds: int32 [4], P('groups'), parts along dimension 0, may hold values from 0 to 1073741823
Outputs:
- mixed: bfloat16 [1024, 2560], P(('groups', 'tensor')), parts along dimension 0
- grad_tokens: bfloat16 [1024, 2560], P(('groups', 'tensor')), parts along dimension 0
- grad_gate: bfloat16 [5120, 13824], P('groups', 'tensor'), parts along dimension 0
- grad_up: bfloat16 [5120, 13824], P('groups', 'tensor'), parts along dimension 0
- grad_down: bfloat16 [27648, 2560], P(('groups', 'tensor')), parts along dimension 0
The draws below stay inside these ranges and needn't reach their ends.
There are 2 independent parts, one for each index of `groups`. The reference program is written for one: setup_inputs(seed, part) draws one part's arguments, and reference() takes and returns one part's arrays. A program takes and returns all parts, laid end to end along the dimension named above; an argument that names none is the same for every part. Nothing has to cross between parts.
All inputs are finite; a program needn't handle non-finite values.
Results may differ from the reference program's by a relative error of at most 0.0061.
Values may be sent and summed in bfloat16 or wider, within the bound.
A program may use at most 192 MiB of HBM per device.

```python
import jax
import jax.numpy as jnp
from jax import lax

D = 2560
FF = 13824
TOK = 512
SHARDS = 16
N_TENSOR = 16


def place_ends(result, own_key, smallest, high):
    longest = result.shape.index(max(result.shape))
    spots = []
    for shift in (0, 1):
        where = [jax.random.randint(jax.random.fold_in(own_key, axis), (), 0, length) for axis, length in enumerate(result.shape)]
        where[longest] = (where[longest] + shift) % result.shape[longest]
        spots.append(tuple(where))
    return result.at[spots[0]].set(smallest).at[spots[1]].set(high)


def block_scale(stream_key, extent, shards, low, top_value):
    def one(dim, blocks):
        steps = jax.random.uniform(jax.random.fold_in(jax.random.fold_in(stream_key, 6), dim), (blocks,), jnp.float32, low / len(shards), top_value / len(shards))
        return jnp.repeat(jnp.exp(steps), extent[dim] // blocks).reshape((-1,) + (1,) * (len(extent) - dim - 1))

    gain = one(*shards[0])
    for cut in shards[1:]:
        gain = gain * one(*cut)
    return gain


def centred(key, extent, width, most, pieces=(), kind=jnp.bfloat16):
    factor_of = block_scale(key, extent, pieces, -0.22, 0.18) if pieces else 1.0
    entries = jax.random.normal(key, extent, jnp.float32) * width * factor_of
    return jnp.minimum(jnp.maximum(entries, -most), most).astype(kind)


def setup_inputs(seed: int = 0, part: int = 0) -> dict:
    keys = jax.random.split(jax.random.key(seed), 11)
    part_splits = jax.random.split(jax.random.fold_in(keys[10], part), 11)
    return {
        "tokens": centred(part_splits[0], (TOK, D), 1.0, 6.0, ((0, 16),)),
        "grad_out": centred(part_splits[1], (TOK, D), 1.0, 6.0, ((0, 16),)),
        "gate_base": centred(keys[2], (D, FF), D ** -0.5, 0.125, ((1, 16),)),
        "up_base": centred(keys[3], (D, FF), D ** -0.5, 0.125, ((1, 16),)),
        "down_base": centred(keys[4], (FF, D), FF ** -0.5, 0.0546875, ((0, 16),)),
        "gate_delta": centred(keys[5], (2, D, FF), (11 * D) ** -0.5, 0.03125, ((2, 16),)),
        "up_delta": centred(keys[6], (2, D, FF), (11 * D) ** -0.5, 0.03125, ((2, 16),)),
        "down_delta": centred(keys[7], (2, FF, D), (11 * FF) ** -0.5, 0.015625, ((1, 16),)),
        "offsets": place_ends(jax.random.randint(keys[8], (3, SHARDS), 0, 1073741824), jax.random.fold_in(keys[8], 1), 0, 1073741823).astype(jnp.int32),
        "seeds": jax.random.randint(part_splits[9], (2,), 0, 1073741824).astype(jnp.int32),
    }


def shifted(value, amount):
    return lax.shift_right_logical(value, jnp.full_like(value, amount))


def kept_entries(number, seed_value):
    mixing = number * jnp.int32(-1640531535) + seed_value * jnp.int32(-2048144777)
    mixing = jnp.bitwise_xor(mixing, shifted(mixing, 15))
    mixing = mixing * jnp.int32(-1028477379)
    mixing = jnp.bitwise_xor(mixing, shifted(mixing, 13))
    mixing = mixing * jnp.int32(668265263)
    mixing = jnp.bitwise_xor(mixing, shifted(mixing, 16))
    return shifted(mixing, 8) % 10 == 0


def combine(base, delta, number, seeds):
    first = jnp.where(kept_entries(number, seeds[0]), delta[0].astype(jnp.float32), jnp.float32(0.0))
    second = jnp.where(kept_entries(number, seeds[1]), delta[1].astype(jnp.float32), jnp.float32(0.0))
    return (base.astype(jnp.float32) + 5.0 * (first + second)).astype(jnp.bfloat16)


def reference(tokens, grad_out, gate_base, up_base, down_base, gate_delta, up_delta, down_delta, offsets, seeds):
    shard_cols = FF // N_TENSOR
    row_ids = lax.broadcasted_iota(jnp.int32, (D, FF), 0)
    col_ids = lax.broadcasted_iota(jnp.int32, (D, FF), 1)
    local_ids = row_ids * shard_cols + col_ids % shard_cols
    owners = col_ids // shard_cols
    gate_w = combine(gate_base, gate_delta, jnp.take(offsets[0], owners) + local_ids, seeds)
    up_w = combine(up_base, up_delta, jnp.take(offsets[1], owners) + local_ids, seeds)
    down_rows = lax.broadcasted_iota(jnp.int32, (FF, D), 0)
    down_cols = lax.broadcasted_iota(jnp.int32, (FF, D), 1)
    down_ids = jnp.take(offsets[2], down_rows // shard_cols) + (down_rows % shard_cols) * D + down_cols
    down_w = combine(down_base, down_delta, down_ids, seeds)
    gate_pre = jnp.dot(tokens, gate_w, preferred_element_type=jnp.float32)
    up_pre = jnp.dot(tokens, up_w, preferred_element_type=jnp.float32)
    sigmoid_gate = jax.nn.sigmoid(gate_pre)
    hidden = (gate_pre * sigmoid_gate * up_pre).astype(jnp.bfloat16)
    mixed = jnp.dot(hidden, down_w, preferred_element_type=jnp.float32).astype(jnp.bfloat16)
    grad_hidden = jnp.dot(grad_out, down_w.T, preferred_element_type=jnp.float32)
    grad_gate_act = (grad_hidden * up_pre * sigmoid_gate * (1.0 + gate_pre * (1.0 - sigmoid_gate))).astype(jnp.bfloat16)
    grad_up_act = (grad_hidden * gate_pre * sigmoid_gate).astype(jnp.bfloat16)
    grad_down = jnp.dot(hidden.T, grad_out, preferred_element_type=jnp.float32).astype(jnp.bfloat16)
    grad_gate = jnp.dot(tokens.T, grad_gate_act, preferred_element_type=jnp.float32).astype(jnp.bfloat16)
    grad_up = jnp.dot(tokens.T, grad_up_act, preferred_element_type=jnp.float32).astype(jnp.bfloat16)
    grad_tokens = (jnp.dot(grad_gate_act, gate_w.T, preferred_element_type=jnp.float32)
                   + jnp.dot(grad_up_act, up_w.T, preferred_element_type=jnp.float32)).astype(jnp.bfloat16)
    return (mixed, grad_tokens, grad_gate, grad_up, grad_down)
```

```python
import functools

import jax
import jax.numpy as jnp
from jax import lax
from jax.experimental import pallas as pl
from jax.experimental.pallas import tpu as pltpu
from jax.sharding import PartitionSpec as P

MESH = pl.DeviceIdType.MESH
MUL_I = -1640531535
MUL_S = -2048144777
TENTH = 429496730
LOW = -(1 << 31)
COLS = 128


def srl(value, amount):
    return lax.shift_right_logical(value, jnp.full_like(value, amount))


def kept(mix):
    mix = mix ^ srl(mix, 15)
    mix = mix * jnp.int32(-1028477379)
    mix = mix ^ srl(mix, 13)
    mix = mix * jnp.int32(668265263)
    mix = mix ^ srl(mix, 16)
    scaled = srl(mix, 8) * jnp.int32(TENTH)
    return (scaled ^ jnp.int32(LOW)) < jnp.int32(TENTH + LOW)


def merge_block(base, delta, out, row_mul, col_mul, start0, start1):
    rows = base.shape[0]
    chunk = next((c for c in (96, 48, 32, 16) if rows % c == 0), rows)
    row_ids = lax.broadcasted_iota(jnp.int32, (chunk, COLS), 0)
    col_ids = lax.broadcasted_iota(jnp.int32, (chunk, COLS), 1)
    ids = row_ids * jnp.int32(row_mul) + col_ids * jnp.int32(col_mul)

    def piece(sel, shift):
        first = jnp.where(kept(ids + (start0 + shift)), delta[0, sel, :].astype(jnp.float32), 0.0)
        second = jnp.where(kept(ids + (start1 + shift)), delta[1, sel, :].astype(jnp.float32), 0.0)
        merged = base[sel, :].astype(jnp.float32) + 5.0 * (first + second)
        out[sel, :] = merged.astype(jnp.bfloat16)

    if chunk == rows:
        piece(slice(None), jnp.int32(0))
    else:
        @pl.loop(0, rows // chunk)
        def _(i):
            piece(pl.ds(pl.multiple_of(i * chunk, chunk), chunk), i * jnp.int32(wrap(chunk * row_mul)))


def wrap(value):
    return (value + (1 << 31)) % (1 << 32) - (1 << 31)


def place(n):
    me = lax.axis_index("tensor")
    return lax.div(me, 4), lax.rem(lax.div(me, 2), 2), lax.rem(me, 2)


def merge_kernel(
    n, offs, seeds, tok, grd, gb, ub, db, gd, ud, dd,
    gw, uw, dw, tok_all, grd_all,
    loc_sem, zs, zr, ys, yr, cs, cr,
):
    nz = n // 4
    step = pl.program_id(0)
    last = tok.shape[1] // COLS - 1
    z, y, c = place(n)
    ins, outs = (tok, grd), (tok_all, grd_all)

    def index(zz, yy, cc):
        return {"tensor": (zz * 2 + yy) * 2 + cc}

    def local(a):
        return pltpu.make_async_copy(ins[a], outs[a].at[z, y, c], loc_sem.at[a])

    def z_send(a, d):
        return pltpu.make_async_remote_copy(
            src_ref=ins[a], dst_ref=outs[a].at[z, y, c], send_sem=zs.at[a, d - 1], recv_sem=zr.at[a, d - 1],
            device_id=index(lax.rem(z + d, nz), y, c), device_id_type=MESH)

    def z_recv(a, d):
        return pltpu.make_async_remote_copy(
            src_ref=ins[a], dst_ref=outs[a].at[lax.rem(z + nz - d, nz), y, c], send_sem=zs.at[a, d - 1],
            recv_sem=zr.at[a, d - 1], device_id=index(lax.rem(z + d, nz), y, c), device_id_type=MESH)

    def y_copy(a, d):
        zz = lax.rem(z + nz - d, nz)
        block = outs[a].at[zz, y, c]
        return pltpu.make_async_remote_copy(
            src_ref=ins[a] if d == 0 else block, dst_ref=block, send_sem=ys.at[a, d], recv_sem=yr.at[a, d],
            device_id=index(z, 1 - y, c), device_id_type=MESH)

    def y_recv(a, d):
        block = outs[a].at[lax.rem(z + nz - d, nz), 1 - y, c]
        return pltpu.make_async_remote_copy(
            src_ref=ins[a], dst_ref=block, send_sem=ys.at[a, d], recv_sem=yr.at[a, d],
            device_id=index(z, 1 - y, c), device_id_type=MESH)

    def c_copy(a):
        part = outs[a].at[:, :, c]
        return pltpu.make_async_remote_copy(
            src_ref=part, dst_ref=part, send_sem=cs.at[a], recv_sem=cr.at[a],
            device_id=index(z, y, 1 - c), device_id_type=MESH)

    def c_recv(a):
        part = outs[a].at[:, :, 1 - c]
        return pltpu.make_async_remote_copy(
            src_ref=part, dst_ref=part, send_sem=cs.at[a], recv_sem=cr.at[a],
            device_id=index(z, y, 1 - c), device_id_type=MESH)

    @pl.when(step == 0)
    def _():
        barrier = pltpu.get_barrier_semaphore()
        for d in range(1, nz):
            pl.semaphore_signal(barrier, inc=1, device_id=index(lax.rem(z + d, nz), y, c), device_id_type=MESH)
        pl.semaphore_signal(barrier, inc=1, device_id=index(z, 1 - y, c), device_id_type=MESH)
        pl.semaphore_signal(barrier, inc=1, device_id=index(z, y, 1 - c), device_id_type=MESH)
        pl.semaphore_wait(barrier, nz + 1)
        for a in range(2):
            local(a).start()
            y_copy(a, 0).start()
            for d in range(1, nz):
                z_send(a, d).start()

    def forward_y(a):
        for d in range(1, nz):
            z_recv(a, d).wait_recv()
            y_copy(a, d).start()

    def forward_c(a):
        local(a).wait()
        for d in range(nz):
            y_recv(a, d).wait_recv()
        c_copy(a).start()

    @pl.when(step == last * 8 // 19)
    def _():
        forward_y(0)

    @pl.when(step == last * 14 // 19)
    def _():
        forward_c(0)

    @pl.when(step == last * 16 // 19)
    def _():
        forward_y(1)

    shard = gb.shape[0]
    seed0 = seeds[0] * jnp.int32(MUL_S)
    seed1 = seeds[1] * jnp.int32(MUL_S)
    for m, (base, delta, out) in enumerate(((gb, gd, gw), (ub, ud, uw), (db, dd, dw))):
        if m < 2:
            row_mul, col_mul = MUL_I, wrap(shard * MUL_I)
        else:
            row_mul, col_mul = wrap(tok.shape[1] * MUL_I), MUL_I
        first = offs[m] * jnp.int32(MUL_I) + step * jnp.int32(wrap(COLS * col_mul))
        merge_block(base, delta, out, row_mul, col_mul, first + seed0, first + seed1)

    @pl.when(step == last)
    def _():
        forward_c(1)
        for a in range(2):
            for d in range(1, nz):
                z_send(a, d).wait_send()
            for d in range(nz):
                y_copy(a, d).wait_send()
            c_copy(a).wait_send()
            c_recv(a).wait_recv()


def merge_and_gather(n, offs, seeds, tok, grd, gb, ub, db, gd, ud, dd):
    shard, width = gb.shape
    nz = n // 4
    plain = pl.BlockSpec((shard, COLS), lambda i: (0, i))
    pair = pl.BlockSpec((2, shard, COLS), lambda i: (0, 0, i))
    smem = pl.BlockSpec(memory_space=pltpu.SMEM)
    anyspace = pl.BlockSpec(memory_space=pl.ANY)
    weight = jax.ShapeDtypeStruct((shard, width), jnp.bfloat16)
    gathered = jax.ShapeDtypeStruct((nz, 2, 2) + tok.shape, tok.dtype)
    dma = pltpu.SemaphoreType.DMA
    return pl.pallas_call(
        functools.partial(merge_kernel, n),
        grid=(width // COLS,),
        in_specs=[smem, smem, anyspace, anyspace, plain, plain, plain, pair, pair, pair],
        out_specs=[plain, plain, plain, anyspace, anyspace],
        out_shape=[weight, weight, weight, gathered, gathered],
        scratch_shapes=[
            dma((2,)), dma((2, nz - 1)), dma((2, nz - 1)), dma((2, nz)), dma((2, nz)), dma((2,)), dma((2,)),
        ],
        compiler_params=pltpu.CompilerParams(
            collective_id=0, has_side_effects=True, vmem_limit_bytes=40 * 1024 * 1024,
            dimension_semantics=("arbitrary",)),
    )(offs, seeds, tok, grd, gb, ub, db, gd, ud, dd)


def scatter_kernel(
    n, parts, part0, part1, out0, out1,
    got_c, sum_c, got_y, sum_y, got_z, cs, cr, ys, yr, zs, zr,
):
    nz = n // 4
    z, y, c = place(n)
    width = out0.shape[1] // parts
    parts_in, outs = (part0, part1), (out0, out1)

    def index(zz, yy, cc):
        return {"tensor": (zz * 2 + yy) * 2 + cc}

    barrier = pltpu.get_barrier_semaphore()
    for d in range(1, nz):
        pl.semaphore_signal(barrier, inc=1, device_id=index(lax.rem(z + d, nz), y, c), device_id_type=MESH)
    pl.semaphore_signal(barrier, inc=1, device_id=index(z, 1 - y, c), device_id_type=MESH)
    pl.semaphore_signal(barrier, inc=1, device_id=index(z, y, 1 - c), device_id_type=MESH)
    pl.semaphore_wait(barrier, nz + 1)

    tasks = [(a, p) for a in range(2) for p in range(parts)]

    def c_copy(t):
        a, p = tasks[t]
        return pltpu.make_async_remote_copy(
            src_ref=parts_in[a].at[:, :, 1 - c, :, pl.ds(p * width, width)], dst_ref=got_c.at[t],
            send_sem=cs.at[t], recv_sem=cr.at[t], device_id=index(z, y, 1 - c), device_id_type=MESH)

    def y_copy(t):
        return pltpu.make_async_remote_copy(
            src_ref=sum_c.at[t, :, 1 - y], dst_ref=got_y.at[t],
            send_sem=ys.at[t], recv_sem=yr.at[t], device_id=index(z, 1 - y, c), device_id_type=MESH)

    def z_copy(t, d):
        zz = lax.rem(z + d, nz)
        return pltpu.make_async_remote_copy(
            src_ref=sum_y.at[t, zz], dst_ref=got_z.at[t, d - 1],
            send_sem=zs.at[t, d - 1], recv_sem=zr.at[t, d - 1], device_id=index(zz, y, c), device_id_type=MESH)

    for t in range(len(tasks)):
        c_copy(t).start()
    for t, (a, p) in enumerate(tasks):
        c_copy(t).wait_recv()

        @pl.loop(0, nz)
        def _(zz):
            for yy in range(2):
                mine = parts_in[a][zz, yy, c, :, pl.ds(p * width, width)].astype(jnp.float32)
                sum_c[t, zz, yy] = (mine + got_c[t, zz, yy].astype(jnp.float32)).astype(jnp.bfloat16)

        y_copy(t).start()
    for t in range(len(tasks)):
        y_copy(t).wait_recv()

        @pl.loop(0, nz)
        def _(zz):
            mine = sum_c[t, zz, y].astype(jnp.float32)
            sum_y[t, zz] = (mine + got_y[t, zz].astype(jnp.float32)).astype(jnp.bfloat16)

        for d in range(1, nz):
            z_copy(t, d).start()
    for t, (a, p) in enumerate(tasks):
        total = sum_y[t, z].astype(jnp.float32)
        for d in range(1, nz):
            z_copy(t, d).wait_recv()
            total = total + got_z[t, d - 1].astype(jnp.float32)
        outs[a][:, pl.ds(p * width, width)] = total.astype(jnp.bfloat16)
    for t in range(len(tasks)):
        c_copy(t).wait_send()
        y_copy(t).wait_send()
        for d in range(1, nz):
            z_copy(t, d).wait_send()


def scatter_sum(n, part0, part1):
    nz = n // 4
    rows, width = part0.shape[0] // n, part0.shape[1]
    parts = 2
    tasks = 2 * parts
    wide = width // parts
    part0 = part0.reshape(nz, 2, 2, rows, width)
    part1 = part1.reshape(nz, 2, 2, rows, width)
    vmem = pl.BlockSpec(memory_space=pltpu.VMEM)
    out = jax.ShapeDtypeStruct((rows, width), jnp.bfloat16)
    dma = pltpu.SemaphoreType.DMA
    return pl.pallas_call(
        functools.partial(scatter_kernel, n, parts),
        in_specs=[vmem, vmem],
        out_specs=[vmem, vmem],
        out_shape=[out, out],
        scratch_shapes=[
            pltpu.VMEM((tasks, nz, 2, rows, wide), jnp.bfloat16),
            pltpu.VMEM((tasks, nz, 2, rows, wide), jnp.bfloat16),
            pltpu.VMEM((tasks, nz, rows, wide), jnp.bfloat16),
            pltpu.VMEM((tasks, nz, rows, wide), jnp.bfloat16),
            pltpu.VMEM((tasks, nz - 1, rows, wide), jnp.bfloat16),
            dma((tasks,)), dma((tasks,)), dma((tasks,)), dma((tasks,)), dma((tasks, nz - 1)), dma((tasks, nz - 1)),
        ],
        compiler_params=pltpu.CompilerParams(
            collective_id=1, has_side_effects=True, vmem_limit_bytes=40 * 1024 * 1024),
    )(part0, part1)


def dot(a, b, da, db):
    return lax.dot_general(a, b, (((da,), (db,)), ((), ())), preferred_element_type=jnp.float32)


def per_device(n, tokens, grad_out, gate_base, up_base, down_base, gate_delta, up_delta, down_delta, offsets, seeds):
    gate_w, up_w, down_w, tok_all, grad_all = merge_and_gather(
        n, offsets[:, 0], seeds, tokens, grad_out, gate_base.T, up_base.T, down_base,
        jnp.swapaxes(gate_delta, 1, 2), jnp.swapaxes(up_delta, 1, 2), down_delta)
    total = n * tokens.shape[0]
    tok_all = tok_all.reshape(total, tokens.shape[1])
    grad_all = grad_all.reshape(total, tokens.shape[1])
    gate_pre = dot(gate_w, tok_all, 1, 1)
    up_pre = dot(up_w, tok_all, 1, 1)
    sigmoid_gate = jax.nn.sigmoid(gate_pre)
    hidden = (gate_pre * sigmoid_gate * up_pre).astype(jnp.bfloat16)
    grad_hidden = dot(down_w, grad_all, 1, 1)
    grad_gate_act = (
        grad_hidden * up_pre * sigmoid_gate * (1.0 + gate_pre * (1.0 - sigmoid_gate))
    ).astype(jnp.bfloat16)
    grad_up_act = (grad_hidden * gate_pre * sigmoid_gate).astype(jnp.bfloat16)
    mixed_part = dot(hidden, down_w, 0, 0).astype(jnp.bfloat16)
    grad_tok_part = (dot(grad_gate_act, gate_w, 0, 0) + dot(grad_up_act, up_w, 0, 0)).astype(jnp.bfloat16)
    mixed, grad_tokens = scatter_sum(n, mixed_part, grad_tok_part)
    grad_down = dot(hidden, grad_all, 1, 0).astype(jnp.bfloat16)
    grad_gate = dot(grad_gate_act, tok_all, 1, 0).astype(jnp.bfloat16)
    grad_up = dot(grad_up_act, tok_all, 1, 0).astype(jnp.bfloat16)
    return mixed, grad_tokens, grad_gate.T, grad_up.T, grad_down


def solution(mesh):
    both = P(("groups", "tensor"), None)
    return jax.shard_map(
        functools.partial(per_device, mesh.shape["tensor"]),
        mesh=mesh,
        in_specs=(
            both, both, P(None, "tensor"), P(None, "tensor"), P("tensor", None),
            P(None, None, "tensor"), P(None, None, "tensor"), P(None, "tensor", None),
            P(None, "tensor"), P("groups"),
        ),
        out_specs=(both, both, P("groups", "tensor"), P("groups", "tensor"), both),
        check_vma=False,
    )
```

```python
import functools

import jax
import jax.numpy as jnp
from jax import lax
from jax.experimental import pallas as pl
from jax.experimental.pallas import tpu as pltpu
from jax.sharding import PartitionSpec as P

MESH = pl.DeviceIdType.MESH
MUL_I = -1640531535
MUL_S = -2048144777
TENTH = 429496730
LOW = -(1 << 31)
COLS = 128


def srl(value, amount):
    return lax.shift_right_logical(value, jnp.full_like(value, amount))


def kept(mix):
    mix = mix ^ srl(mix, 15)
    mix = mix * jnp.int32(-1028477379)
    mix = mix ^ srl(mix, 13)
    mix = mix * jnp.int32(668265263)
    mix = mix ^ srl(mix, 16)
    scaled = srl(mix, 8) * jnp.int32(TENTH)
    return (scaled ^ jnp.int32(LOW)) < jnp.int32(TENTH + LOW)


def merge_block(base, delta, out, row_mul, col_mul, start0, start1):
    rows = base.shape[0]
    chunk = next((c for c in (96, 48, 32, 16) if rows % c == 0), rows)
    row_ids = lax.broadcasted_iota(jnp.int32, (chunk, COLS), 0)
    col_ids = lax.broadcasted_iota(jnp.int32, (chunk, COLS), 1)
    ids = row_ids * jnp.int32(row_mul) + col_ids * jnp.int32(col_mul)

    def piece(sel, shift):
        first = jnp.where(kept(ids + (start0 + shift)), delta[0, sel, :].astype(jnp.float32), 0.0)
        second = jnp.where(kept(ids + (start1 + shift)), delta[1, sel, :].astype(jnp.float32), 0.0)
        merged = base[sel, :].astype(jnp.float32) + 5.0 * (first + second)
        out[sel, :] = merged.astype(jnp.bfloat16)

    if chunk == rows:
        piece(slice(None), jnp.int32(0))
    else:
        @pl.loop(0, rows // chunk)
        def _(i):
            piece(pl.ds(pl.multiple_of(i * chunk, chunk), chunk), i * jnp.int32(wrap(chunk * row_mul)))


def wrap(value):
    return (value + (1 << 31)) % (1 << 32) - (1 << 31)


def place(n):
    me = lax.axis_index("tensor")
    return lax.div(me, 4), lax.rem(lax.div(me, 2), 2), lax.rem(me, 2)


def merge_kernel(
    n, offs, seeds, tok, grd, gb, ub, db, gd, ud, dd,
    gw, uw, dw, tok_all, grd_all,
    loc_sem, zs, zr, ys, yr, cs, cr,
):
    nz = n // 4
    step = pl.program_id(0)
    last = tok.shape[1] // COLS - 1
    z, y, c = place(n)
    ins, outs = (tok, grd), (tok_all, grd_all)

    def index(zz, yy, cc):
        return {"tensor": (zz * 2 + yy) * 2 + cc}

    def local(a):
        return pltpu.make_async_copy(ins[a], outs[a].at[z, y, c], loc_sem.at[a])

    def z_send(a, d):
        return pltpu.make_async_remote_copy(
            src_ref=ins[a], dst_ref=outs[a].at[z, y, c], send_sem=zs.at[a, d - 1], recv_sem=zr.at[a, d - 1],
            device_id=index(lax.rem(z + d, nz), y, c), device_id_type=MESH)

    def z_recv(a, d):
        return pltpu.make_async_remote_copy(
            src_ref=ins[a], dst_ref=outs[a].at[lax.rem(z + nz - d, nz), y, c], send_sem=zs.at[a, d - 1],
            recv_sem=zr.at[a, d - 1], device_id=index(lax.rem(z + d, nz), y, c), device_id_type=MESH)

    def y_copy(a, d):
        zz = lax.rem(z + nz - d, nz)
        block = outs[a].at[zz, y, c]
        return pltpu.make_async_remote_copy(
            src_ref=ins[a] if d == 0 else block, dst_ref=block, send_sem=ys.at[a, d], recv_sem=yr.at[a, d],
            device_id=index(z, 1 - y, c), device_id_type=MESH)

    def y_recv(a, d):
        block = outs[a].at[lax.rem(z + nz - d, nz), 1 - y, c]
        return pltpu.make_async_remote_copy(
            src_ref=ins[a], dst_ref=block, send_sem=ys.at[a, d], recv_sem=yr.at[a, d],
            device_id=index(z, 1 - y, c), device_id_type=MESH)

    def c_copy(a):
        part = outs[a].at[:, :, c]
        return pltpu.make_async_remote_copy(
            src_ref=part, dst_ref=part, send_sem=cs.at[a], recv_sem=cr.at[a],
            device_id=index(z, y, 1 - c), device_id_type=MESH)

    def c_recv(a):
        part = outs[a].at[:, :, 1 - c]
        return pltpu.make_async_remote_copy(
            src_ref=part, dst_ref=part, send_sem=cs.at[a], recv_sem=cr.at[a],
            device_id=index(z, y, 1 - c), device_id_type=MESH)

    @pl.when(step == 0)
    def _():
        barrier = pltpu.get_barrier_semaphore()
        for d in range(1, nz):
            pl.semaphore_signal(barrier, inc=1, device_id=index(lax.rem(z + d, nz), y, c), device_id_type=MESH)
        pl.semaphore_signal(barrier, inc=1, device_id=index(z, 1 - y, c), device_id_type=MESH)
        pl.semaphore_signal(barrier, inc=1, device_id=index(z, y, 1 - c), device_id_type=MESH)
        pl.semaphore_wait(barrier, nz + 1)
        for a in range(2):
            local(a).start()
            y_copy(a, 0).start()
            for d in range(1, nz):
                z_send(a, d).start()

    def forward_y(a):
        for d in range(1, nz):
            z_recv(a, d).wait_recv()
            y_copy(a, d).start()

    def forward_c(a):
        local(a).wait()
        for d in range(nz):
            y_recv(a, d).wait_recv()
        c_copy(a).start()

    @pl.when(step == last * 8 // 19)
    def _():
        forward_y(0)

    @pl.when(step == last * 14 // 19)
    def _():
        forward_c(0)

    @pl.when(step == last * 16 // 19)
    def _():
        forward_y(1)

    shard = gb.shape[0]
    seed0 = seeds[0] * jnp.int32(MUL_S)
    seed1 = seeds[1] * jnp.int32(MUL_S)
    for m, (base, delta, out) in enumerate(((gb, gd, gw), (ub, ud, uw), (db, dd, dw))):
        if m < 2:
            row_mul, col_mul = MUL_I, wrap(shard * MUL_I)
        else:
            row_mul, col_mul = wrap(tok.shape[1] * MUL_I), MUL_I
        first = offs[m] * jnp.int32(MUL_I) + step * jnp.int32(wrap(COLS * col_mul))
        merge_block(base, delta, out, row_mul, col_mul, first + seed0, first + seed1)

    @pl.when(step == last)
    def _():
        forward_c(1)
        for a in range(2):
            for d in range(1, nz):
                z_send(a, d).wait_send()
            for d in range(nz):
                y_copy(a, d).wait_send()
            c_copy(a).wait_send()
            c_recv(a).wait_recv()


def merge_and_gather(n, offs, seeds, tok, grd, gb, ub, db, gd, ud, dd):
    shard, width = gb.shape
    nz = n // 4
    plain = pl.BlockSpec((shard, COLS), lambda i: (0, i))
    pair = pl.BlockSpec((2, shard, COLS), lambda i: (0, 0, i))
    smem = pl.BlockSpec(memory_space=pltpu.SMEM)
    anyspace = pl.BlockSpec(memory_space=pl.ANY)
    weight = jax.ShapeDtypeStruct((shard, width), jnp.bfloat16)
    gathered = jax.ShapeDtypeStruct((nz, 2, 2) + tok.shape, tok.dtype)
    dma = pltpu.SemaphoreType.DMA
    return pl.pallas_call(
        functools.partial(merge_kernel, n),
        grid=(width // COLS,),
        in_specs=[smem, smem, anyspace, anyspace, plain, plain, plain, pair, pair, pair],
        out_specs=[plain, plain, plain, anyspace, anyspace],
        out_shape=[weight, weight, weight, gathered, gathered],
        scratch_shapes=[
            dma((2,)), dma((2, nz - 1)), dma((2, nz - 1)), dma((2, nz)), dma((2, nz)), dma((2,)), dma((2,)),
        ],
        compiler_params=pltpu.CompilerParams(
            collective_id=0, has_side_effects=True, vmem_limit_bytes=40 * 1024 * 1024,
            dimension_semantics=("arbitrary",)),
    )(offs, seeds, tok, grd, gb, ub, db, gd, ud, dd)


def dot(a, b, da, db):
    return lax.dot_general(a, b, (((da,), (db,)), ((), ())), preferred_element_type=jnp.float32)


TILE = 256


def finish_kernel(
    n, parts, hid_in, ga_in, ua_in, gw_in, uw_in, dw_in, tok_in, grd_in,
    out0, out1, grad_gate, grad_up, grad_down,
    hid, ga, ua, gw, uw, dw, tok, grd, part0, part1, stage,
    got_c, sum_c, got_y, sum_y, got_z, load_sem, stage_sem, cs, cr, ys, yr, zs, zr,
):
    nz = n // 4
    z, y, c = place(n)
    width = out0.shape[1] // parts
    rows = out0.shape[0]
    parts_in, outs = (part0, part1), (out0, out1)

    def index(zz, yy, cc):
        return {"tensor": (zz * 2 + yy) * 2 + cc}

    loads = [
        pltpu.make_async_copy(src, dst, load_sem.at[i])
        for i, (src, dst) in enumerate((
            (hid_in, hid), (dw_in, dw), (ga_in, ga), (ua_in, ua), (gw_in, gw), (uw_in, uw), (grd_in, grd), (tok_in, tok)))
    ]
    for load in loads:
        load.start()

    barrier = pltpu.get_barrier_semaphore()
    for d in range(1, nz):
        pl.semaphore_signal(barrier, inc=1, device_id=index(lax.rem(z + d, nz), y, c), device_id_type=MESH)
    pl.semaphore_signal(barrier, inc=1, device_id=index(z, 1 - y, c), device_id_type=MESH)
    pl.semaphore_signal(barrier, inc=1, device_id=index(z, y, 1 - c), device_id_type=MESH)
    pl.semaphore_wait(barrier, nz + 1)

    tasks = [(a, p) for a in range(2) for p in range(parts)]

    def c_copy(t):
        a, p = tasks[t]
        return pltpu.make_async_remote_copy(
            src_ref=parts_in[a].at[:, :, 1 - c, :, pl.ds(p * width, width)], dst_ref=got_c.at[t],
            send_sem=cs.at[t], recv_sem=cr.at[t], device_id=index(z, y, 1 - c), device_id_type=MESH)

    def y_copy(t):
        return pltpu.make_async_remote_copy(
            src_ref=sum_c.at[t, :, 1 - y], dst_ref=got_y.at[t],
            send_sem=ys.at[t], recv_sem=yr.at[t], device_id=index(z, 1 - y, c), device_id_type=MESH)

    def z_copy(t, d):
        zz = lax.rem(z + d, nz)
        return pltpu.make_async_remote_copy(
            src_ref=sum_y.at[t, zz], dst_ref=got_z.at[t, d - 1],
            send_sem=zs.at[t, d - 1], recv_sem=zr.at[t, d - 1], device_id=index(zz, y, c), device_id_type=MESH)

    def core_step(t):
        a, p = tasks[t]
        c_copy(t).wait_recv()

        @pl.loop(0, nz)
        def _(zz):
            for yy in range(2):
                mine = parts_in[a][zz, yy, c, :, pl.ds(p * width, width)].astype(jnp.float32)
                sum_c[t, zz, yy] = (mine + got_c[t, zz, yy].astype(jnp.float32)).astype(jnp.bfloat16)

        y_copy(t).start()

    def y_step(t):
        y_copy(t).wait_recv()

        @pl.loop(0, nz)
        def _(zz):
            mine = sum_c[t, zz, y].astype(jnp.float32)
            sum_y[t, zz] = (mine + got_y[t, zz].astype(jnp.float32)).astype(jnp.bfloat16)

        for d in range(1, nz):
            z_copy(t, d).start()

    def z_step(t):
        a, p = tasks[t]
        total = sum_y[t, z].astype(jnp.float32)
        for d in range(1, nz):
            z_copy(t, d).wait_recv()
            total = total + got_z[t, d - 1].astype(jnp.float32)
        outs[a][:, pl.ds(p * width, width)] = total.astype(jnp.bfloat16)

    def partial_sums(t, pairs):
        a, p = tasks[t]

        @pl.loop(0, width // TILE)
        def _(i):
            cols = pl.ds(pl.multiple_of(p * width + i * TILE, TILE), TILE)
            total = dot(pairs[0][0][...], pairs[0][1][:, cols], 0, 0)
            for left, right in pairs[1:]:
                total = total + dot(left[...], right[:, cols], 0, 0)
            parts_in[a][:, :, :, :, cols] = total.reshape(nz, 2, 2, rows, TILE).astype(jnp.bfloat16)

        c_copy(t).start()

    def weight_grad(left, right, out, used):
        @pl.loop(0, out.shape[1] // (2 * TILE))
        def _(i):
            for slot in range(2):
                cols = pl.ds(pl.multiple_of((2 * i + slot) * TILE, TILE), TILE)
                copy = pltpu.make_async_copy(stage.at[slot], out.at[:, cols], stage_sem.at[slot])
                if used:
                    copy.wait()
                else:
                    @pl.when(i > 0)
                    def _():
                        copy.wait()
                stage[slot] = dot(left[...], right[:, cols], 1, 0).astype(jnp.bfloat16)
                copy.start()

    loads[0].wait()
    loads[1].wait()
    partial_sums(0, [(hid, dw)])
    partial_sums(1, [(hid, dw)])
    core_step(0)
    for load in loads[2:6]:
        load.wait()
    partial_sums(2, [(ga, gw), (ua, uw)])
    core_step(1)
    partial_sums(3, [(ga, gw), (ua, uw)])
    core_step(2)
    loads[6].wait()
    loads[7].wait()
    y_step(0)
    core_step(3)
    weight_grad(hid, grd, grad_down, False)
    y_step(1)
    weight_grad(ga, tok, grad_gate, True)
    y_step(2)
    weight_grad(ua, tok, grad_up, True)
    y_step(3)
    for slot in range(2):
        pltpu.make_async_copy(stage.at[slot], grad_up.at[:, pl.ds(0, TILE)], stage_sem.at[slot]).wait()
    for t in range(len(tasks)):
        z_step(t)
    for t in range(len(tasks)):
        c_copy(t).wait_send()
        y_copy(t).wait_send()
        for d in range(1, nz):
            z_copy(t, d).wait_send()


def finish(n, hid, ga, ua, gw, uw, dw, tok, grd):
    nz = n // 4
    total, width = tok.shape
    rows = total // n
    parts = 2
    tasks = 2 * parts
    wide = width // parts
    vmem = pl.BlockSpec(memory_space=pltpu.VMEM)
    anyspace = pl.BlockSpec(memory_space=pl.ANY)
    out = jax.ShapeDtypeStruct((rows, width), jnp.bfloat16)
    grad = jax.ShapeDtypeStruct(gw.shape, jnp.bfloat16)
    dma = pltpu.SemaphoreType.DMA
    arrays = (hid, ga, ua, gw, uw, dw, tok, grd)
    return pl.pallas_call(
        functools.partial(finish_kernel, n, parts),
        in_specs=[anyspace] * 8,
        out_specs=[vmem, vmem, anyspace, anyspace, anyspace],
        out_shape=[out, out, grad, grad, grad],
        scratch_shapes=[pltpu.VMEM(x.shape, x.dtype) for x in arrays] + [
            pltpu.VMEM((nz, 2, 2, rows, width), jnp.bfloat16),
            pltpu.VMEM((nz, 2, 2, rows, width), jnp.bfloat16),
            pltpu.VMEM((2, gw.shape[0], TILE), jnp.bfloat16),
            pltpu.VMEM((tasks, nz, 2, rows, wide), jnp.bfloat16),
            pltpu.VMEM((tasks, nz, 2, rows, wide), jnp.bfloat16),
            pltpu.VMEM((tasks, nz, rows, wide), jnp.bfloat16),
            pltpu.VMEM((tasks, nz, rows, wide), jnp.bfloat16),
            pltpu.VMEM((tasks, nz - 1, rows, wide), jnp.bfloat16),
            dma((8,)), dma((2,)),
            dma((tasks,)), dma((tasks,)), dma((tasks,)), dma((tasks,)), dma((tasks, nz - 1)), dma((tasks, nz - 1)),
        ],
        compiler_params=pltpu.CompilerParams(
            collective_id=1, has_side_effects=True, vmem_limit_bytes=48 * 1024 * 1024),
    )(*arrays)


def per_device(n, tokens, grad_out, gate_base, up_base, down_base, gate_delta, up_delta, down_delta, offsets, seeds):
    gate_w, up_w, down_w, tok_all, grad_all = merge_and_gather(
        n, offsets[:, 0], seeds, tokens, grad_out, gate_base.T, up_base.T, down_base,
        jnp.swapaxes(gate_delta, 1, 2), jnp.swapaxes(up_delta, 1, 2), down_delta)
    total = n * tokens.shape[0]
    tok_all = tok_all.reshape(total, tokens.shape[1])
    grad_all = grad_all.reshape(total, tokens.shape[1])
    gate_pre = dot(gate_w, tok_all, 1, 1)
    up_pre = dot(up_w, tok_all, 1, 1)
    sigmoid_gate = jax.nn.sigmoid(gate_pre)
    hidden = (gate_pre * sigmoid_gate * up_pre).astype(jnp.bfloat16)
    grad_hidden = dot(down_w, grad_all, 1, 1)
    grad_gate_act = (
        grad_hidden * up_pre * sigmoid_gate * (1.0 + gate_pre * (1.0 - sigmoid_gate))
    ).astype(jnp.bfloat16)
    grad_up_act = (grad_hidden * gate_pre * sigmoid_gate).astype(jnp.bfloat16)
    mixed, grad_tokens, grad_gate, grad_up, grad_down = finish(
        n, hidden, grad_gate_act, grad_up_act, gate_w, up_w, down_w, tok_all, grad_all)
    return mixed, grad_tokens, grad_gate.T, grad_up.T, grad_down


def solution(mesh):
    both = P(("groups", "tensor"), None)
    return jax.shard_map(
        functools.partial(per_device, mesh.shape["tensor"]),
        mesh=mesh,
        in_specs=(
            both, both, P(None, "tensor"), P(None, "tensor"), P("tensor", None),
            P(None, None, "tensor"), P(None, None, "tensor"), P(None, "tensor", None),
            P(None, "tensor"), P("groups"),
        ),
        out_specs=(both, both, P("groups", "tensor"), P("groups", "tensor"), both),
        check_vma=False,
    )
```

```python
import functools

import jax
import jax.numpy as jnp
from jax import lax
from jax.experimental import pallas as pl
from jax.experimental.pallas import tpu as pltpu
from jax.sharding import PartitionSpec as P

MESH = pl.DeviceIdType.MESH
MUL_I = -1640531535
MUL_S = -2048144777
TENTH = 429496730
LOW = -(1 << 31)
COLS = 128


def srl(value, amount):
    return lax.shift_right_logical(value, jnp.full_like(value, amount))


def kept(mix):
    mix = mix ^ srl(mix, 15)
    mix = mix * jnp.int32(-1028477379)
    mix = mix ^ srl(mix, 13)
    mix = mix * jnp.int32(668265263)
    mix = mix ^ srl(mix, 16)
    scaled = srl(mix, 8) * jnp.int32(TENTH)
    return (scaled ^ jnp.int32(LOW)) < jnp.int32(TENTH + LOW)


def merge_block(base, delta, out, row_mul, col_mul, start0, start1):
    rows = base.shape[0]
    chunk = next((c for c in (96, 48, 32, 16) if rows % c == 0), rows)
    row_ids = lax.broadcasted_iota(jnp.int32, (chunk, COLS), 0)
    col_ids = lax.broadcasted_iota(jnp.int32, (chunk, COLS), 1)
    ids = row_ids * jnp.int32(row_mul) + col_ids * jnp.int32(col_mul)

    def piece(sel, shift):
        first = jnp.where(kept(ids + (start0 + shift)), delta[0, sel, :].astype(jnp.float32), 0.0)
        second = jnp.where(kept(ids + (start1 + shift)), delta[1, sel, :].astype(jnp.float32), 0.0)
        merged = base[sel, :].astype(jnp.float32) + 5.0 * (first + second)
        out[sel, :] = merged.astype(jnp.bfloat16)

    if chunk == rows:
        piece(slice(None), jnp.int32(0))
    else:
        @pl.loop(0, rows // chunk)
        def _(i):
            piece(pl.ds(pl.multiple_of(i * chunk, chunk), chunk), i * jnp.int32(wrap(chunk * row_mul)))


def wrap(value):
    return (value + (1 << 31)) % (1 << 32) - (1 << 31)


def place(n):
    me = lax.axis_index("tensor")
    return lax.div(me, 4), lax.rem(lax.div(me, 2), 2), lax.rem(me, 2)


def merge_kernel(
    n, offs, seeds, tok, grd, gb, ub, db, gd, ud, dd,
    gw, uw, dw, tok_all, grd_all,
    loc_sem, zs, zr, ys, yr, cs, cr,
):
    nz = n // 4
    step = pl.program_id(0)
    last = tok.shape[1] // COLS - 1
    z, y, c = place(n)
    ins, outs = (tok, grd), (tok_all, grd_all)

    def index(zz, yy, cc):
        return {"tensor": (zz * 2 + yy) * 2 + cc}

    def local(a):
        return pltpu.make_async_copy(ins[a], outs[a].at[z, y, c], loc_sem.at[a])

    def z_send(a, d):
        return pltpu.make_async_remote_copy(
            src_ref=ins[a], dst_ref=outs[a].at[z, y, c], send_sem=zs.at[a, d - 1], recv_sem=zr.at[a, d - 1],
            device_id=index(lax.rem(z + d, nz), y, c), device_id_type=MESH)

    def z_recv(a, d):
        return pltpu.make_async_remote_copy(
            src_ref=ins[a], dst_ref=outs[a].at[lax.rem(z + nz - d, nz), y, c], send_sem=zs.at[a, d - 1],
            recv_sem=zr.at[a, d - 1], device_id=index(lax.rem(z + d, nz), y, c), device_id_type=MESH)

    def y_copy(a, d):
        zz = lax.rem(z + nz - d, nz)
        block = outs[a].at[zz, y, c]
        return pltpu.make_async_remote_copy(
            src_ref=ins[a] if d == 0 else block, dst_ref=block, send_sem=ys.at[a, d], recv_sem=yr.at[a, d],
            device_id=index(z, 1 - y, c), device_id_type=MESH)

    def y_recv(a, d):
        block = outs[a].at[lax.rem(z + nz - d, nz), 1 - y, c]
        return pltpu.make_async_remote_copy(
            src_ref=ins[a], dst_ref=block, send_sem=ys.at[a, d], recv_sem=yr.at[a, d],
            device_id=index(z, 1 - y, c), device_id_type=MESH)

    def c_copy(a):
        part = outs[a].at[:, :, c]
        return pltpu.make_async_remote_copy(
            src_ref=part, dst_ref=part, send_sem=cs.at[a], recv_sem=cr.at[a],
            device_id=index(z, y, 1 - c), device_id_type=MESH)

    def c_recv(a):
        part = outs[a].at[:, :, 1 - c]
        return pltpu.make_async_remote_copy(
            src_ref=part, dst_ref=part, send_sem=cs.at[a], recv_sem=cr.at[a],
            device_id=index(z, y, 1 - c), device_id_type=MESH)

    @pl.when(step == 0)
    def _():
        barrier = pltpu.get_barrier_semaphore()
        for d in range(1, nz):
            pl.semaphore_signal(barrier, inc=1, device_id=index(lax.rem(z + d, nz), y, c), device_id_type=MESH)
        pl.semaphore_signal(barrier, inc=1, device_id=index(z, 1 - y, c), device_id_type=MESH)
        pl.semaphore_signal(barrier, inc=1, device_id=index(z, y, 1 - c), device_id_type=MESH)
        pl.semaphore_wait(barrier, nz + 1)
        for a in range(2):
            local(a).start()
            y_copy(a, 0).start()
            for d in range(1, nz):
                z_send(a, d).start()

    def forward_y(a):
        for d in range(1, nz):
            z_recv(a, d).wait_recv()
            y_copy(a, d).start()

    def forward_c(a):
        local(a).wait()
        for d in range(nz):
            y_recv(a, d).wait_recv()
        c_copy(a).start()

    @pl.when(step == last * 8 // 19)
    def _():
        forward_y(0)

    @pl.when(step == last * 13 // 19)
    def _():
        forward_y(1)

    @pl.when(step == last * 16 // 19)
    def _():
        forward_c(0)

    shard = gb.shape[0]
    seed0 = seeds[0] * jnp.int32(MUL_S)
    seed1 = seeds[1] * jnp.int32(MUL_S)
    for m, (base, delta, out) in enumerate(((gb, gd, gw), (ub, ud, uw), (db, dd, dw))):
        if m < 2:
            row_mul, col_mul = MUL_I, wrap(shard * MUL_I)
        else:
            row_mul, col_mul = wrap(tok.shape[1] * MUL_I), MUL_I
        first = offs[m] * jnp.int32(MUL_I) + step * jnp.int32(wrap(COLS * col_mul))
        merge_block(base, delta, out, row_mul, col_mul, first + seed0, first + seed1)

    @pl.when(step == last)
    def _():
        forward_c(1)
        for a in range(2):
            for d in range(1, nz):
                z_send(a, d).wait_send()
            for d in range(nz):
                y_copy(a, d).wait_send()
            c_copy(a).wait_send()
            c_recv(a).wait_recv()


def merge_and_gather(n, offs, seeds, tok, grd, gb, ub, db, gd, ud, dd):
    shard, width = gb.shape
    nz = n // 4
    plain = pl.BlockSpec((shard, COLS), lambda i: (0, i))
    pair = pl.BlockSpec((2, shard, COLS), lambda i: (0, 0, i))
    smem = pl.BlockSpec(memory_space=pltpu.SMEM)
    anyspace = pl.BlockSpec(memory_space=pl.ANY)
    weight = jax.ShapeDtypeStruct((shard, width), jnp.bfloat16)
    gathered = jax.ShapeDtypeStruct((nz, 2, 2) + tok.shape, tok.dtype)
    dma = pltpu.SemaphoreType.DMA
    return pl.pallas_call(
        functools.partial(merge_kernel, n),
        grid=(width // COLS,),
        in_specs=[smem, smem, anyspace, anyspace, plain, plain, plain, pair, pair, pair],
        out_specs=[plain, plain, plain, anyspace, anyspace],
        out_shape=[weight, weight, weight, gathered, gathered],
        scratch_shapes=[
            dma((2,)), dma((2, nz - 1)), dma((2, nz - 1)), dma((2, nz)), dma((2, nz)), dma((2,)), dma((2,)),
        ],
        compiler_params=pltpu.CompilerParams(
            collective_id=0, has_side_effects=True, vmem_limit_bytes=40 * 1024 * 1024,
            dimension_semantics=("arbitrary",)),
    )(offs, seeds, tok, grd, gb, ub, db, gd, ud, dd)


def dot(a, b, da, db):
    return lax.dot_general(a, b, (((da,), (db,)), ((), ())), preferred_element_type=jnp.float32)


TILE = 256


def finish_kernel(
    n, parts, hid_in, ga_in, ua_in, gw_in, uw_in, dw_in, tok_in, grd_in,
    out0, out1, grad_gate, grad_up, grad_down,
    hid, ga, ua, gw, uw, dw, tok, grd, hid_t, ga_t, ua_t, part0, part1, stage,
    got_c, sum_c, got_y, sum_y, got_z, load_sem, stage_sem, cs, cr, ys, yr, zs, zr,
):
    nz = n // 4
    z, y, c = place(n)
    width = out0.shape[1] // parts
    rows = out0.shape[0]
    parts_in, outs = (part0, part1), (out0, out1)

    def index(zz, yy, cc):
        return {"tensor": (zz * 2 + yy) * 2 + cc}

    loads = [
        pltpu.make_async_copy(src, dst, load_sem.at[i])
        for i, (src, dst) in enumerate((
            (hid_in, hid), (dw_in, dw), (ga_in, ga), (ua_in, ua), (gw_in, gw), (uw_in, uw), (grd_in, grd), (tok_in, tok)))
    ]
    for load in loads:
        load.start()

    barrier = pltpu.get_barrier_semaphore()
    for d in range(1, nz):
        pl.semaphore_signal(barrier, inc=1, device_id=index(lax.rem(z + d, nz), y, c), device_id_type=MESH)
    pl.semaphore_signal(barrier, inc=1, device_id=index(z, 1 - y, c), device_id_type=MESH)
    pl.semaphore_signal(barrier, inc=1, device_id=index(z, y, 1 - c), device_id_type=MESH)
    pl.semaphore_wait(barrier, nz + 1)

    tasks = [(a, p) for a in range(2) for p in range(parts)]

    def c_copy(t):
        a, p = tasks[t]
        return pltpu.make_async_remote_copy(
            src_ref=parts_in[a].at[:, :, 1 - c, :, pl.ds(p * width, width)], dst_ref=got_c.at[t],
            send_sem=cs.at[t], recv_sem=cr.at[t], device_id=index(z, y, 1 - c), device_id_type=MESH)

    def y_copy(t):
        return pltpu.make_async_remote_copy(
            src_ref=sum_c.at[t, :, 1 - y], dst_ref=got_y.at[t],
            send_sem=ys.at[t], recv_sem=yr.at[t], device_id=index(z, 1 - y, c), device_id_type=MESH)

    def z_copy(t, d):
        zz = lax.rem(z + d, nz)
        return pltpu.make_async_remote_copy(
            src_ref=sum_y.at[t, zz], dst_ref=got_z.at[t, d - 1],
            send_sem=zs.at[t, d - 1], recv_sem=zr.at[t, d - 1], device_id=index(zz, y, c), device_id_type=MESH)

    def core_step(t):
        a, p = tasks[t]
        c_copy(t).wait_recv()

        @pl.loop(0, nz)
        def _(zz):
            for yy in range(2):
                mine = parts_in[a][zz, yy, c, :, pl.ds(p * width, width)].astype(jnp.float32)
                sum_c[t, zz, yy] = (mine + got_c[t, zz, yy].astype(jnp.float32)).astype(jnp.bfloat16)

        y_copy(t).start()

    def y_step(t):
        y_copy(t).wait_recv()

        @pl.loop(0, nz)
        def _(zz):
            mine = sum_c[t, zz, y].astype(jnp.float32)
            sum_y[t, zz] = (mine + got_y[t, zz].astype(jnp.float32)).astype(jnp.bfloat16)

        for d in range(1, nz):
            z_copy(t, d).start()

    def z_step(t):
        a, p = tasks[t]
        total = sum_y[t, z].astype(jnp.float32)
        for d in range(1, nz):
            z_copy(t, d).wait_recv()
            total = total + got_z[t, d - 1].astype(jnp.float32)
        outs[a][:, pl.ds(p * width, width)] = total.astype(jnp.bfloat16)

    def partial_sums(t, pairs):
        a, p = tasks[t]

        @pl.loop(0, width // TILE)
        def _(i):
            cols = pl.ds(pl.multiple_of(p * width + i * TILE, TILE), TILE)
            total = dot(pairs[0][0][...], pairs[0][1][:, cols], 1, 0)
            for left, right in pairs[1:]:
                total = total + dot(left[...], right[:, cols], 1, 0)
            parts_in[a][:, :, :, :, cols] = total.reshape(nz, 2, 2, rows, TILE).astype(jnp.bfloat16)

        c_copy(t).start()

    def weight_grad(left, right, out, used):
        @pl.loop(0, out.shape[1] // (2 * TILE))
        def _(i):
            for slot in range(2):
                cols = pl.ds(pl.multiple_of((2 * i + slot) * TILE, TILE), TILE)
                copy = pltpu.make_async_copy(stage.at[slot], out.at[:, cols], stage_sem.at[slot])
                if used:
                    copy.wait()
                else:
                    @pl.when(i > 0)
                    def _():
                        copy.wait()
                stage[slot] = dot(left[...], right[:, cols], 1, 0).astype(jnp.bfloat16)
                copy.start()

    loads[0].wait()
    loads[1].wait()
    hid_t[...] = hid[...].T
    partial_sums(0, [(hid_t, dw)])
    partial_sums(1, [(hid_t, dw)])
    core_step(0)
    for load in loads[2:6]:
        load.wait()
    ga_t[...] = ga[...].T
    ua_t[...] = ua[...].T
    partial_sums(2, [(ga_t, gw), (ua_t, uw)])
    core_step(1)
    partial_sums(3, [(ga_t, gw), (ua_t, uw)])
    core_step(2)
    loads[6].wait()
    loads[7].wait()
    y_step(0)
    core_step(3)
    weight_grad(hid, grd, grad_down, False)
    y_step(1)
    weight_grad(ga, tok, grad_gate, True)
    y_step(2)
    weight_grad(ua, tok, grad_up, True)
    y_step(3)
    for slot in range(2):
        pltpu.make_async_copy(stage.at[slot], grad_up.at[:, pl.ds(0, TILE)], stage_sem.at[slot]).wait()
    for t in range(len(tasks)):
        z_step(t)
    for t in range(len(tasks)):
        c_copy(t).wait_send()
        y_copy(t).wait_send()
        for d in range(1, nz):
            z_copy(t, d).wait_send()


def finish(n, hid, ga, ua, gw, uw, dw, tok, grd):
    nz = n // 4
    total, width = tok.shape
    rows = total // n
    parts = 2
    tasks = 2 * parts
    wide = width // parts
    vmem = pl.BlockSpec(memory_space=pltpu.VMEM)
    anyspace = pl.BlockSpec(memory_space=pl.ANY)
    out = jax.ShapeDtypeStruct((rows, width), jnp.bfloat16)
    grad = jax.ShapeDtypeStruct(gw.shape, jnp.bfloat16)
    dma = pltpu.SemaphoreType.DMA
    arrays = (hid, ga, ua, gw, uw, dw, tok, grd)
    return pl.pallas_call(
        functools.partial(finish_kernel, n, parts),
        in_specs=[anyspace] * 8,
        out_specs=[vmem, vmem, anyspace, anyspace, anyspace],
        out_shape=[out, out, grad, grad, grad],
        scratch_shapes=[pltpu.VMEM(x.shape, x.dtype) for x in arrays] + [
            pltpu.VMEM(hid.shape[::-1], hid.dtype),
            pltpu.VMEM(hid.shape[::-1], hid.dtype),
            pltpu.VMEM(hid.shape[::-1], hid.dtype),
            pltpu.VMEM((nz, 2, 2, rows, width), jnp.bfloat16),
            pltpu.VMEM((nz, 2, 2, rows, width), jnp.bfloat16),
            pltpu.VMEM((2, gw.shape[0], TILE), jnp.bfloat16),
            pltpu.VMEM((tasks, nz, 2, rows, wide), jnp.bfloat16),
            pltpu.VMEM((tasks, nz, 2, rows, wide), jnp.bfloat16),
            pltpu.VMEM((tasks, nz, rows, wide), jnp.bfloat16),
            pltpu.VMEM((tasks, nz, rows, wide), jnp.bfloat16),
            pltpu.VMEM((tasks, nz - 1, rows, wide), jnp.bfloat16),
            dma((8,)), dma((2,)),
            dma((tasks,)), dma((tasks,)), dma((tasks,)), dma((tasks,)), dma((tasks, nz - 1)), dma((tasks, nz - 1)),
        ],
        compiler_params=pltpu.CompilerParams(
            collective_id=1, has_side_effects=True, vmem_limit_bytes=48 * 1024 * 1024),
    )(*arrays)


def per_device(n, tokens, grad_out, gate_base, up_base, down_base, gate_delta, up_delta, down_delta, offsets, seeds):
    gate_w, up_w, down_w, tok_all, grad_all = merge_and_gather(
        n, offsets[:, 0], seeds, tokens, grad_out, gate_base.T, up_base.T, down_base,
        jnp.swapaxes(gate_delta, 1, 2), jnp.swapaxes(up_delta, 1, 2), down_delta)
    total = n * tokens.shape[0]
    tok_all = tok_all.reshape(total, tokens.shape[1])
    grad_all = grad_all.reshape(total, tokens.shape[1])
    gate_pre = dot(gate_w, tok_all, 1, 1)
    up_pre = dot(up_w, tok_all, 1, 1)
    sigmoid_gate = jax.nn.sigmoid(gate_pre)
    hidden = (gate_pre * sigmoid_gate * up_pre).astype(jnp.bfloat16)
    grad_hidden = dot(down_w, grad_all, 1, 1)
    grad_gate_act = (
        grad_hidden * up_pre * sigmoid_gate * (1.0 + gate_pre * (1.0 - sigmoid_gate))
    ).astype(jnp.bfloat16)
    grad_up_act = (grad_hidden * gate_pre * sigmoid_gate).astype(jnp.bfloat16)
    mixed, grad_tokens, grad_gate, grad_up, grad_down = finish(
        n, hidden, grad_gate_act, grad_up_act, gate_w, up_w, down_w, tok_all, grad_all)
    return mixed, grad_tokens, grad_gate.T, grad_up.T, grad_down


def solution(mesh):
    both = P(("groups", "tensor"), None)
    return jax.shard_map(
        functools.partial(per_device, mesh.shape["tensor"]),
        mesh=mesh,
        in_specs=(
            both, both, P(None, "tensor"), P(None, "tensor"), P("tensor", None),
            P(None, None, "tensor"), P(None, None, "tensor"), P(None, "tensor", None),
            P(None, "tensor"), P("groups"),
        ),
        out_specs=(both, both, P("groups", "tensor"), P("groups", "tensor"), both),
        check_vma=False,
    )
```
